512 devices in a mesh: context: 32 (over x, z_hi, core), dp: 16 (over z_lo, y).
Axes of the slice: x: 4, y: 8, z: 8 (z_hi: 4, z_lo: 2; z = z_hi * 2 + z_lo), core: 2. Of those that a mesh axis runs over, the one named last changes fastest.
Arguments:
- hyena_in: bfloat16 [32768, 4096], P(('dp', 'context')), parts along dimension 0, may hold values from -6 to 6
- filt: bfloat16 [32768, 128], P(('dp', 'context')), parts along dimension 0, may hold values from -1 to 1
- keys: bfloat16 [32768, 4096], P(('dp', 'context')), parts along dimension 0, may hold values from -81 to 81
- values: bfloat16 [32768, 4096], P(('dp', 'context')), parts along dimension 0, may hold values from -6 to 6
Outputs:
- mixed: bfloat16 [32768, 4096], P(('dp', 'context')), parts along dimension 0
The draws below stay inside these ranges and needn't reach their ends.
There are 16 independent parts, one for each index of `dp`. The reference program is written for one: setup_inputs(seed, part) draws one part's arguments, and reference() takes and returns one part's arrays. A program takes and returns all parts, laid end to end along the dimension named above; each array names one. Nothing has to cross between parts.
All inputs are finite; a program needn't handle non-finite values.
Results may differ from the reference program's by a relative error of at most 0.0089.
Values may be sent and summed in bfloat16 or wider, within the bound.
No kernel may reach another device: no remote copies, remote signals or barrier semaphores. Data moves between devices by JAX's collectives and lax.ppermute only.
A program may use at most 64 MiB of HBM per device.

```python
import jax
import jax.numpy as jnp
from jax import lax

TOK_DEV = 64
HEAD_DIM = 128
GROUPS = 128
C = 4096
SEQ = 2048


def draw_filt(key, part):
    key = jax.random.fold_in(key, 1)
    key_rate, key_noise = jax.random.split(key, 2)
    low = jnp.log(0.5 / SEQ)
    high = jnp.log(1.0 / 40.0)
    rates = jnp.exp(jax.random.uniform(key_rate, (1, GROUPS), jnp.float32, low, high))
    steps = jnp.arange(SEQ, dtype=jnp.float32)[:, None]
    noise = jnp.clip(jax.random.normal(key_noise, (SEQ, GROUPS), jnp.float32), -4.0, 4.0)
    return (noise * jnp.sqrt(2.0 * rates) * jnp.exp(-rates * steps)).astype(jnp.bfloat16)


def draw_keys(key, part):
    key = jax.random.fold_in(key, 2)
    key_base = jax.random.fold_in(key, 0)
    return jnp.clip(jax.random.normal(key_base, (SEQ, C), jnp.float32), -4.0, 4.0).astype(jnp.bfloat16)


def block_scale(stream_key, extent, cuts, low, largest):
    def one(dim, parts):
        draws = jax.random.uniform(jax.random.fold_in(jax.random.fold_in(stream_key, 6), dim), (parts,), jnp.float32, low / len(cuts), largest / len(cuts))
        return jnp.repeat(jnp.exp(draws), extent[dim] // parts).reshape((-1,) + (1,) * (len(extent) - dim - 1))

    loudness = one(*cuts[0])
    for cut in cuts[1:]:
        loudness = loudness * one(*cut)
    return loudness


def gaussian(rng, shape, scale, reach, cuts=(), kind=jnp.bfloat16):
    entries = scale * jax.random.normal(rng, shape, jnp.float32)
    if cuts:
        entries = entries * block_scale(rng, shape, cuts, -0.22, 0.18)
    return jnp.clip(entries, -reach, reach).astype(kind)


def setup_inputs(seed: int = 0, part: int = 0) -> dict:
    key_list = jax.random.split(jax.random.key(seed), 5)
    own_keys = jax.random.split(jax.random.fold_in(key_list[4], part), 5)
    return {
        "hyena_in": gaussian(own_keys[0], (SEQ, C), 1.0, 6.0, ((0, 32),)),
        "filt": draw_filt(jax.random.fold_in(jax.random.fold_in(key_list[4], part), 71), part),
        "keys": draw_keys(jax.random.fold_in(jax.random.fold_in(key_list[4], part), 71), part),
        "values": gaussian(own_keys[3], (SEQ, C), 1.0, 6.0, ((0, 32),)),
    }


def reference(hyena_in, filt, keys, values):
    seq, width = hyena_in.shape
    groups = filt.shape[1]
    total = 2 * seq
    spec = jnp.fft.fft(hyena_in.astype(jnp.float32), n=total, axis=0)
    fspec = jnp.fft.fft(filt.astype(jnp.float32), n=total, axis=0)
    fspec = jnp.tile(fspec, (1, width // groups))
    conv = jnp.real(jnp.fft.ifft(spec * fspec, axis=0))[:seq].astype(jnp.float32)
    queries = conv.astype(jnp.bfloat16)
    block = TOK_DEV
    heads = width // HEAD_DIM
    scale = 1.0 / (HEAD_DIM ** 0.5)
    zeros = jnp.zeros((2 * block, width), keys.dtype)
    key_pad = jnp.concatenate([zeros, keys], axis=0)
    val_pad = jnp.concatenate([zeros, values], axis=0)
    nblocks = seq // block

    def one_block(index):
        start = (index * block).astype(jnp.int32)
        query_blk = lax.dynamic_slice_in_dim(queries, start, block, 0).reshape(block, heads, HEAD_DIM)
        key_blk = lax.dynamic_slice_in_dim(key_pad, start, 3 * block, 0).reshape(3 * block, heads, HEAD_DIM)
        val_blk = lax.dynamic_slice_in_dim(val_pad, start, 3 * block, 0).reshape(3 * block, heads, HEAD_DIM)
        scores = jnp.einsum("qhd,khd->hqk", query_blk.astype(jnp.float32), key_blk.astype(jnp.float32)) * scale
        rows = jnp.arange(block, dtype=jnp.int32)[:, None]
        cols = jnp.arange(3 * block, dtype=jnp.int32)[None, :]
        allowed = (cols >= (2 - index) * block) & (cols <= 2 * block + rows)
        scores = jnp.where(allowed[None], scores, -1e30)
        top = jnp.max(scores, axis=-1, keepdims=True)
        expo = jnp.where(allowed[None], jnp.exp(scores - top), 0.0)
        probs = (expo / jnp.sum(expo, axis=-1, keepdims=True)).astype(jnp.bfloat16)
        out = jnp.einsum("hqk,khd->qhd", probs.astype(jnp.float32), val_blk.astype(jnp.float32))
        return out.astype(jnp.bfloat16).reshape(block, width)

    outs = lax.map(one_block, jnp.arange(nblocks, dtype=jnp.int32))
    return outs.reshape(seq, width)
```

```python
import functools
import math

import jax
import jax.numpy as jnp
import ml_dtypes
import numpy as np
from jax import lax
from jax.experimental import pallas as pl
from jax.experimental.pallas import tpu as pltpu
from jax.sharding import PartitionSpec as P

HEAD_DIM = 128
BLOCK = 256
TILE = 128
VMEM_LIMIT = 48 * 1024 * 1024


def bf16_parts(table, count):
    parts = []
    rest = table.astype(np.float64)
    for _ in range(count):
        part = rest.astype(np.float32).astype(ml_dtypes.bfloat16)
        parts.append(part)
        rest = rest - part.astype(np.float64)
    return np.stack(parts)


def forward_table():
    freq = np.arange(BLOCK)[:, None] + 0.5
    angle = freq * np.arange(BLOCK)[None, :] * (math.pi / BLOCK)
    return np.concatenate([np.cos(angle), -np.sin(angle)], axis=0)


def inverse_table():
    freq = np.arange(BLOCK)[None, :] + 0.5
    angle = freq * (BLOCK + np.arange(BLOCK))[:, None] * (math.pi / BLOCK)
    return np.concatenate([np.cos(angle), -np.sin(angle)], axis=1) / BLOCK


def dot(left, right):
    return lax.dot_general(
        left, right, (((1,), (0,)), ((), ())), preferred_element_type=jnp.float32
    )


def pack_kernel(x_ref, k_ref, v_ref, out_ref):
    tok, width = x_ref.shape
    for head in range(width // HEAD_DIM):
        cols = slice(head * HEAD_DIM, (head + 1) * HEAD_DIM)
        for place, ref in enumerate((x_ref, k_ref, v_ref)):
            out_ref[head, place * tok : (place + 1) * tok, :] = ref[:, cols]


def filter_kernel(me_ref, filt_ref, table_ref, out_ref):
    blocks, _, _ = out_ref.shape
    tok = filt_ref.shape[2]
    per = BLOCK // tok
    me = me_ref[0]
    sign = 1.0 - 2.0 * (lax.broadcasted_iota(jnp.int32, (BLOCK, 1), 0) % 2).astype(jnp.float32)
    before_re = jnp.zeros((BLOCK, HEAD_DIM), jnp.float32)
    before_im = before_re
    for block in range(blocks):
        pieces = []
        for part in range(per):
            place = lax.bitwise_xor(me, jnp.int32(block * per + part))
            pieces.append(filt_ref[lax.bitwise_and(place, 1), lax.shift_right_logical(place, 1)])
        chunk = jnp.concatenate(pieces, axis=0)
        spec = dot(table_ref[0], chunk) + dot(table_ref[1], chunk)
        spec_re, spec_im = spec[:BLOCK], spec[BLOCK:]
        out_ref[block, :BLOCK, :] = before_re + sign * spec_im
        out_ref[block, BLOCK:, :] = before_im - sign * spec_re
        before_re, before_im = spec_re, spec_im


def main_kernel(y_ref, w_ref, fwd_ref, inv_ref, out_ref, spec, total_hi, total_lo, queries):
    sources, _, width = y_ref.shape
    tok = out_ref.shape[1]
    per = BLOCK // tok
    blocks = sources // per
    for pair in range(blocks // 2):
        both = jnp.concatenate(
            [
                y_ref[block * per : (block + 1) * per, :tok, :].reshape(BLOCK, width)
                for block in (2 * pair, 2 * pair + 1)
            ],
            axis=1,
        )
        got = dot(fwd_ref[0], both) + dot(fwd_ref[1], both)
        spec[2 * pair] = got[:, :width]
        spec[2 * pair + 1] = got[:, width:]

    def products(step, carry):
        low = pl.ds(pl.multiple_of(step * 8, 8), 8)
        high = pl.ds(pl.multiple_of(step * 8 + BLOCK, 8), 8)
        x_re = [spec[block, low, :] for block in range(blocks)]
        x_im = [spec[block, high, :] for block in range(blocks)]
        w_re = [w_ref[block, low, :] for block in range(blocks)]
        w_im = [w_ref[block, high, :] for block in range(blocks)]
        for block in range(blocks):
            re = im = None
            for first in range(block + 1):
                a, b = x_re[first], x_im[first]
                c, d = w_re[block - first], w_im[block - first]
                new_re, new_im = a * c - b * d, a * d + b * c
                re = new_re if re is None else re + new_re
                im = new_im if im is None else im + new_im
            spec[block, low, :] = re
            spec[block, high, :] = im
        return carry

    lax.fori_loop(0, BLOCK // 8, products, 0)
    for block in range(blocks):
        value = spec[block]
        hi = value.astype(jnp.bfloat16)
        cols = slice(block * width, (block + 1) * width)
        total_hi[:, cols] = hi
        total_lo[:, cols] = (value - hi.astype(jnp.float32)).astype(jnp.bfloat16)
    for pair in range(blocks // 2):
        cols = slice(2 * pair * width, (2 * pair + 2) * width)
        hi, lo = total_hi[:, cols], total_lo[:, cols]
        conv = dot(inv_ref[0], hi) + (dot(inv_ref[0], lo) + dot(inv_ref[1], hi))
        conv = conv.astype(jnp.bfloat16)
        queries[2 * pair * BLOCK : (2 * pair + 1) * BLOCK, :] = conv[:, :width]
        queries[(2 * pair + 1) * BLOCK : (2 * pair + 2) * BLOCK, :] = conv[:, width:]

    reach = TILE // tok
    factor = math.log2(math.e) / math.sqrt(HEAD_DIM)
    for tile in range(sources // reach):
        first = max(tile * reach - reach, 0)
        last = (tile + 1) * reach
        span = (last - first) * tok
        ahead = tile * TILE - first * tok
        key = y_ref[first:last, tok : 2 * tok, :].reshape(span, width)
        val = y_ref[first:last, 2 * tok : 3 * tok, :].reshape(span, width)
        query = queries[tile * TILE : (tile + 1) * TILE, :]
        scores = lax.dot_general(
            query, key, (((1,), (1,)), ((), ())), preferred_element_type=jnp.float32
        )
        row = lax.broadcasted_iota(jnp.int32, (TILE, span), 0)
        col = lax.broadcasted_iota(jnp.int32, (TILE, span), 1)
        allowed = (col <= row + ahead) & (col >= row // tok * tok + ahead - 2 * tok)
        scores = jnp.where(allowed, scores, -1e30)
        top = jnp.max(scores, axis=-1, keepdims=True)
        expo = jnp.exp2((scores - top) * factor)
        probs = (expo * (1.0 / jnp.sum(expo, axis=-1, keepdims=True))).astype(jnp.bfloat16)
        mixed = dot(probs, val).astype(jnp.bfloat16)
        out_ref[tile * reach : last] = mixed.reshape(reach, tok, width)


def gather_filt(filt):
    held = filt[None]
    peers = lax.axis_size("context")
    bit = 2
    while bit < peers:
        other = lax.ppermute(held, "context", [(i, i ^ bit) for i in range(peers)])
        held = jnp.concatenate([held, other], axis=0)
        bit *= 2
    other = lax.ppermute(held, "context", [(i, i ^ 1) for i in range(peers)])
    return jnp.stack([held, other])


def vmem(count):
    return [pl.BlockSpec(memory_space=pltpu.VMEM)] * count


def local(hyena_in, filt, keys, values):
    peers = lax.axis_size("context")
    tok, width = hyena_in.shape
    blocks = peers * tok // BLOCK
    params = pltpu.CompilerParams(vmem_limit_bytes=VMEM_LIMIT)
    fwd = jnp.asarray(bf16_parts(forward_table(), 2))
    inv = jnp.asarray(bf16_parts(inverse_table(), 2))
    me = lax.axis_index("context").astype(jnp.int32).reshape(1)

    packed = pl.pallas_call(
        pack_kernel,
        out_shape=jax.ShapeDtypeStruct((peers, 3 * tok, HEAD_DIM), jnp.bfloat16),
        in_specs=vmem(3),
        out_specs=vmem(1)[0],
        compiler_params=params,
        cost_estimate=pl.CostEstimate(flops=0, bytes_accessed=6 * tok * width * 2, transcendentals=0),
        name="pack",
    )(hyena_in, keys, values)
    moved = lax.all_to_all(packed, "context", split_axis=0, concat_axis=0, tiled=True)

    all_filt = gather_filt(filt)
    spectra = pl.pallas_call(
        filter_kernel,
        out_shape=jax.ShapeDtypeStruct((blocks, 2 * BLOCK, HEAD_DIM), jnp.float32),
        in_specs=[pl.BlockSpec(memory_space=pltpu.SMEM)] + vmem(2),
        out_specs=vmem(1)[0],
        compiler_params=params,
        cost_estimate=pl.CostEstimate(
            flops=blocks * 8 * BLOCK * BLOCK * HEAD_DIM, bytes_accessed=4 << 20, transcendentals=0
        ),
        name="filter_spectra",
    )(me, all_filt, fwd)

    mixed = pl.pallas_call(
        main_kernel,
        out_shape=jax.ShapeDtypeStruct((peers, tok, HEAD_DIM), jnp.bfloat16),
        in_specs=vmem(4),
        out_specs=vmem(1)[0],
        scratch_shapes=[
            pltpu.VMEM((blocks, 2 * BLOCK, HEAD_DIM), jnp.float32),
            pltpu.VMEM((2 * BLOCK, blocks * HEAD_DIM), jnp.bfloat16),
            pltpu.VMEM((2 * BLOCK, blocks * HEAD_DIM), jnp.bfloat16),
            pltpu.VMEM((peers * tok, HEAD_DIM), jnp.bfloat16),
        ],
        compiler_params=params,
        cost_estimate=pl.CostEstimate(flops=4 << 30, bytes_accessed=5 << 20, transcendentals=1 << 19),
        name="conv_attention",
    )(moved, spectra, fwd, inv)
    home = lax.all_to_all(mixed, "context", split_axis=0, concat_axis=0, tiled=True)
    return home.transpose(1, 0, 2).reshape(tok, width)


def solution(mesh):
    spec = P(("dp", "context"), None)
    return jax.shard_map(
        local, mesh=mesh, in_specs=(spec,) * 4, out_specs=spec, check_vma=False
    )
```

```python
import math

import jax
import jax.numpy as jnp
import ml_dtypes
import numpy as np
from jax import lax
from jax.experimental import pallas as pl
from jax.experimental.pallas import tpu as pltpu
from jax.sharding import PartitionSpec as P

HEAD_DIM = 128
BLOCK = 256
TILE = 128
VMEM_LIMIT = 48 * 1024 * 1024
CHUNKS = 4


def bf16_parts(table, count):
    parts = []
    rest = table.astype(np.float64)
    for _ in range(count):
        part = rest.astype(np.float32).astype(ml_dtypes.bfloat16)
        parts.append(part)
        rest = rest - part.astype(np.float64)
    return np.stack(parts)


def forward_table():
    freq = np.arange(BLOCK)[:, None] + 0.5
    angle = freq * np.arange(BLOCK)[None, :] * (math.pi / BLOCK)
    return np.concatenate([np.cos(angle), -np.sin(angle)], axis=0)


def inverse_table():
    freq = np.arange(BLOCK)[None, :] + 0.5
    angle = freq * (BLOCK + np.arange(BLOCK))[:, None] * (math.pi / BLOCK)
    return np.concatenate([np.cos(angle), -np.sin(angle)], axis=1) / BLOCK


def dot(left, right):
    return lax.dot_general(
        left, right, (((1,), (0,)), ((), ())), preferred_element_type=jnp.float32
    )


def copy(src, dst, sem):
    return pltpu.make_async_copy(src, dst, sem)


def pack_kernel(x_ref, k_ref, v_ref, f_ref, out_ref, held, half, load, store):
    tok, width = x_ref.shape
    heads = width // HEAD_DIM
    group = heads // CHUNKS
    part = tok // 2
    filters = copy(f_ref, half, load.at[CHUNKS])
    filters.start()
    loads = [[] for _ in range(CHUNKS)]
    for head in range(heads):
        cols = pl.ds(head * HEAD_DIM, HEAD_DIM)
        for place, ref in enumerate((x_ref, k_ref, v_ref)):
            step = copy(
                ref.at[:, cols], held.at[head, pl.ds(place * tok, tok)], load.at[head // group]
            )
            step.start()
            loads[head // group].append(step)
    filters.wait()
    for head in range(heads):
        first = head % 2 * part
        held[head, 3 * tok :, :] = half[first : first + part, :]
    stores = []
    for chunk in range(CHUNKS):
        for step in loads[chunk]:
            step.wait()
        some = pl.ds(chunk * group, group)
        step = copy(held.at[some], out_ref.at[some], store.at[chunk])
        step.start()
        stores.append(step)
    for step in stores:
        step.wait()


def pack(hyena_in, keys, values, filt):
    tok, width = hyena_in.shape
    heads = width // HEAD_DIM
    shape = (heads, 3 * tok + tok // 2, HEAD_DIM)
    anywhere = pl.BlockSpec(memory_space=pl.ANY)
    return pl.pallas_call(
        pack_kernel,
        out_shape=jax.ShapeDtypeStruct(shape, jnp.bfloat16),
        in_specs=[anywhere] * 4,
        out_specs=anywhere,
        scratch_shapes=[
            pltpu.VMEM(shape, jnp.bfloat16),
            pltpu.VMEM((tok, HEAD_DIM), jnp.bfloat16),
            pltpu.SemaphoreType.DMA((CHUNKS + 1,)),
            pltpu.SemaphoreType.DMA((CHUNKS,)),
        ],
        cost_estimate=pl.CostEstimate(
            flops=0, bytes_accessed=14 * tok * width, transcendentals=0
        ),
        name="pack",
    )(hyena_in, keys, values, filt)


def main_kernel(
    me_ref, y_ref, other_ref, fwd_ref, inv_ref, out_ref, spec, fspec, filt, bias, queries
):
    sources, _, width = y_ref.shape
    tok = out_ref.shape[1]
    half = tok // 2
    per = BLOCK // tok
    blocks = sources // per
    odd = lax.bitwise_and(me_ref[0], 1)
    for source in range(sources):
        at = pl.multiple_of(source * tok + odd * half, half)
        filt[pl.ds(at, half), :] = y_ref[source, 3 * tok : 3 * tok + half, :]
        at = pl.multiple_of(source * tok + (1 - odd) * half, half)
        filt[pl.ds(at, half), :] = other_ref[source]

    for pair in range(blocks // 2):
        x_both = jnp.concatenate(
            [
                y_ref[block * per : (block + 1) * per, :tok, :].reshape(BLOCK, width)
                for block in (2 * pair, 2 * pair + 1)
            ],
            axis=1,
        )
        f_both = jnp.concatenate(
            [
                filt[block * BLOCK : (block + 1) * BLOCK, :]
                for block in (2 * pair, 2 * pair + 1)
            ],
            axis=1,
        )
        for both, result in ((x_both, spec), (f_both, fspec)):
            got = dot(fwd_ref[0], both) + dot(fwd_ref[1], both)
            result[2 * pair] = got[:, :width]
            result[2 * pair + 1] = got[:, width:]

    sign = 1.0 - 2.0 * (lax.broadcasted_iota(jnp.int32, (8, width), 0) % 2).astype(jnp.float32)

    def products(step, carry):
        low = pl.ds(pl.multiple_of(step * 8, 8), 8)
        high = pl.ds(pl.multiple_of(step * 8 + BLOCK, 8), 8)
        x_re = [spec[block, low, :] for block in range(blocks)]
        x_im = [spec[block, high, :] for block in range(blocks)]
        x_sum = [re + im for re, im in zip(x_re, x_im)]
        f_re = [fspec[block, low, :] for block in range(blocks)]
        f_im = [fspec[block, high, :] for block in range(blocks)]
        w_re, w_im = [], []
        for block in range(blocks):
            re, im = sign * f_im[block], -sign * f_re[block]
            w_re.append(re + f_re[block - 1] if block else re)
            w_im.append(im + f_im[block - 1] if block else im)
        w_sum = [re + im for re, im in zip(w_re, w_im)]
        for block in range(blocks):
            p = q = r = None
            for first in range(block + 1):
                other = block - first
                p_new = x_re[first] * w_re[other]
                q_new = x_im[first] * w_im[other]
                r_new = x_sum[first] * w_sum[other]
                p = p_new if p is None else p + p_new
                q = q_new if q is None else q + q_new
                r = r_new if r is None else r + r_new
            spec[block, low, :] = p - q
            spec[block, high, :] = r - (p + q)
        return carry

    lax.fori_loop(0, BLOCK // 8, products, 0, unroll=4)
    for pair in range(blocks // 2):
        value = jnp.concatenate([spec[2 * pair], spec[2 * pair + 1]], axis=1)
        hi = value.astype(jnp.bfloat16)
        lo = (value - hi.astype(jnp.float32)).astype(jnp.bfloat16)
        conv = dot(inv_ref[0], hi) + (dot(inv_ref[0], lo) + dot(inv_ref[1], hi))
        conv = conv.astype(jnp.bfloat16)
        queries[2 * pair * BLOCK : (2 * pair + 1) * BLOCK, :] = conv[:, :width]
        queries[(2 * pair + 1) * BLOCK : (2 * pair + 2) * BLOCK, :] = conv[:, width:]

    reach = TILE // tok
    factor = math.log2(math.e) / math.sqrt(HEAD_DIM)
    row = lax.broadcasted_iota(jnp.int32, (TILE, 2 * TILE), 0)
    col = lax.broadcasted_iota(jnp.int32, (TILE, 2 * TILE), 1)
    allowed = (col <= row + TILE) & (col >= row // tok * tok)
    bias[...] = jnp.where(allowed, 0.0, -1e30)
    for tile in range(sources // reach):
        first = max(tile * reach - reach, 0)
        last = (tile + 1) * reach
        span = (last - first) * tok
        key = y_ref[first:last, tok : 2 * tok, :].reshape(span, width)
        val = y_ref[first:last, 2 * tok : 3 * tok, :].reshape(span, width)
        query = queries[tile * TILE : (tile + 1) * TILE, :]
        scores = lax.dot_general(
            query, key, (((1,), (1,)), ((), ())), preferred_element_type=jnp.float32
        )
        scores = scores + bias[:, 2 * TILE - span :]
        top = jnp.max(scores, axis=-1, keepdims=True)
        expo = jnp.exp2((scores - top) * factor)
        probs = (expo * (1.0 / jnp.sum(expo, axis=-1, keepdims=True))).astype(jnp.bfloat16)
        mixed = dot(probs, val).astype(jnp.bfloat16)
        out_ref[tile * reach : last] = mixed.reshape(reach, tok, width)


def vmem(count):
    return [pl.BlockSpec(memory_space=pltpu.VMEM)] * count


def local(hyena_in, filt, keys, values):
    peers = lax.axis_size("context")
    tok, width = hyena_in.shape
    blocks = peers * tok // BLOCK
    fwd = jnp.asarray(bf16_parts(forward_table(), 2))
    inv = jnp.asarray(bf16_parts(inverse_table(), 2))
    me = lax.axis_index("context").astype(jnp.int32).reshape(1)

    packed = pack(hyena_in, keys, values, filt)
    moved = lax.all_to_all(packed, "context", split_axis=0, concat_axis=0, tiled=True)
    other = lax.ppermute(moved[:, 3 * tok :], "context", [(i, i ^ 1) for i in range(peers)])

    mixed = pl.pallas_call(
        main_kernel,
        out_shape=jax.ShapeDtypeStruct((peers, tok, HEAD_DIM), jnp.bfloat16),
        in_specs=[pl.BlockSpec(memory_space=pltpu.SMEM)] + vmem(4),
        out_specs=vmem(1)[0],
        scratch_shapes=[
            pltpu.VMEM((blocks, 2 * BLOCK, HEAD_DIM), jnp.float32),
            pltpu.VMEM((blocks, 2 * BLOCK, HEAD_DIM), jnp.float32),
            pltpu.VMEM((peers * tok, HEAD_DIM), jnp.bfloat16),
            pltpu.VMEM((TILE, 2 * TILE), jnp.float32),
            pltpu.VMEM((peers * tok, HEAD_DIM), jnp.bfloat16),
        ],
        compiler_params=pltpu.CompilerParams(vmem_limit_bytes=VMEM_LIMIT),
        cost_estimate=pl.CostEstimate(flops=5 << 30, bytes_accessed=5 << 20, transcendentals=1 << 19),
        name="conv_attention",
    )(me, moved, other, fwd, inv)
    home = lax.all_to_all(mixed, "context", split_axis=0, concat_axis=0, tiled=True)
    return home.transpose(1, 0, 2).reshape(tok, width)


def solution(mesh):
    spec = P(("dp", "context"), None)
    return jax.shard_map(
        local, mesh=mesh, in_specs=(spec,) * 4, out_specs=spec, check_vma=False
    )
```

```python
import math

import jax
import jax.numpy as jnp
import ml_dtypes
import numpy as np
from jax import lax
from jax.experimental import pallas as pl
from jax.experimental.pallas import tpu as pltpu
from jax.sharding import PartitionSpec as P

HEAD_DIM = 128
BLOCK = 256
TILE = 128
VMEM_LIMIT = 48 * 1024 * 1024
CHUNKS = 4


def bf16_parts(table, count):
    parts = []
    rest = table.astype(np.float64)
    for _ in range(count):
        part = rest.astype(np.float32).astype(ml_dtypes.bfloat16)
        parts.append(part)
        rest = rest - part.astype(np.float64)
    return np.stack(parts)


def forward_table():
    freq = np.arange(BLOCK)[:, None] + 0.5
    angle = freq * np.arange(BLOCK)[None, :] * (math.pi / BLOCK)
    return np.concatenate([np.cos(angle), -np.sin(angle)], axis=0)


def inverse_table():
    freq = np.arange(BLOCK)[None, :] + 0.5
    angle = freq * (BLOCK + np.arange(BLOCK))[:, None] * (math.pi / BLOCK)
    return np.concatenate([np.cos(angle), -np.sin(angle)], axis=1) / BLOCK


def dot(left, right):
    return lax.dot_general(
        left, right, (((1,), (0,)), ((), ())), preferred_element_type=jnp.float32
    )


def copy(src, dst, sem):
    return pltpu.make_async_copy(src, dst, sem)


def pack_kernel(x_ref, k_ref, v_ref, f_ref, out_ref, held, half, load, store):
    tok, width = x_ref.shape
    heads = width // HEAD_DIM
    group = heads // CHUNKS
    part = tok // 2
    filters = copy(f_ref, half, load.at[CHUNKS])
    filters.start()
    loads = [[] for _ in range(CHUNKS)]
    for head in range(heads):
        cols = pl.ds(head * HEAD_DIM, HEAD_DIM)
        for place, ref in enumerate((x_ref, k_ref, v_ref)):
            step = copy(
                ref.at[:, cols], held.at[head, pl.ds(place * tok, tok)], load.at[head // group]
            )
            step.start()
            loads[head // group].append(step)
    filters.wait()
    for head in range(heads):
        first = head % 2 * part
        held[head, 3 * tok :, :] = half[first : first + part, :]
    stores = []
    for chunk in range(CHUNKS):
        for step in loads[chunk]:
            step.wait()
        some = pl.ds(chunk * group, group)
        step = copy(held.at[some], out_ref.at[some], store.at[chunk])
        step.start()
        stores.append(step)
    for step in stores:
        step.wait()


def pack(hyena_in, keys, values, filt):
    tok, width = hyena_in.shape
    heads = width // HEAD_DIM
    shape = (heads, 3 * tok + tok // 2, HEAD_DIM)
    anywhere = pl.BlockSpec(memory_space=pl.ANY)
    return pl.pallas_call(
        pack_kernel,
        out_shape=jax.ShapeDtypeStruct(shape, jnp.bfloat16),
        in_specs=[anywhere] * 4,
        out_specs=anywhere,
        scratch_shapes=[
            pltpu.VMEM(shape, jnp.bfloat16),
            pltpu.VMEM((tok, HEAD_DIM), jnp.bfloat16),
            pltpu.SemaphoreType.DMA((CHUNKS + 1,)),
            pltpu.SemaphoreType.DMA((CHUNKS,)),
        ],
        cost_estimate=pl.CostEstimate(
            flops=0, bytes_accessed=14 * tok * width, transcendentals=0
        ),
        name="pack",
    )(hyena_in, keys, values, filt)


def spectra_kernel(y_ref, fwd_ref, spec):
    sources, _, width = y_ref.shape
    tok = BLOCK // 4
    half = tok // 2
    per = BLOCK // tok
    blocks = sources // per
    for pair in range(blocks // 2):
        x_both = jnp.concatenate(
            [
                y_ref[block * per : (block + 1) * per, :tok, :].reshape(BLOCK, width)
                for block in (2 * pair, 2 * pair + 1)
            ],
            axis=1,
        )
        got = dot(fwd_ref[...], jnp.concatenate([x_both, x_both], axis=0))
        spec[2 * pair] = got[:, :width]
        spec[2 * pair + 1] = got[:, width:]


def main_kernel(
    me_ref, y_ref, other_ref, spec, fwd_ref, inv_ref, out_ref, total, fspec, filt, bias, queries
):
    sources, _, width = y_ref.shape
    tok = out_ref.shape[1]
    half = tok // 2
    per = BLOCK // tok
    blocks = sources // per
    odd = lax.bitwise_and(me_ref[0], 1)
    for source in range(sources):
        at = pl.multiple_of(source * tok + odd * half, half)
        filt[pl.ds(at, half), :] = y_ref[source, 3 * tok : 3 * tok + half, :]
        at = pl.multiple_of(source * tok + (1 - odd) * half, half)
        filt[pl.ds(at, half), :] = other_ref[source]

    for pair in range(blocks // 2):
        both = jnp.concatenate(
            [
                filt[block * BLOCK : (block + 1) * BLOCK, :]
                for block in (2 * pair, 2 * pair + 1)
            ],
            axis=1,
        )
        got = dot(fwd_ref[...], jnp.concatenate([both, both], axis=0))
        fspec[2 * pair] = got[:, :width]
        fspec[2 * pair + 1] = got[:, width:]

    sign = 1.0 - 2.0 * (lax.broadcasted_iota(jnp.int32, (8, width), 0) % 2).astype(jnp.float32)

    def products(step, carry):
        low = pl.ds(pl.multiple_of(step * 8, 8), 8)
        high = pl.ds(pl.multiple_of(step * 8 + BLOCK, 8), 8)
        x_re = [spec[block, low, :] for block in range(blocks)]
        x_im = [spec[block, high, :] for block in range(blocks)]
        x_sum = [re + im for re, im in zip(x_re, x_im)]
        f_re = [fspec[block, low, :] for block in range(blocks)]
        f_im = [fspec[block, high, :] for block in range(blocks)]
        w_re, w_im = [], []
        for block in range(blocks):
            re, im = sign * f_im[block], -sign * f_re[block]
            w_re.append(re + f_re[block - 1] if block else re)
            w_im.append(im + f_im[block - 1] if block else im)
        w_sum = [re + im for re, im in zip(w_re, w_im)]
        for block in range(blocks):
            p = q = r = None
            for first in range(block + 1):
                other = block - first
                p_new = x_re[first] * w_re[other]
                q_new = x_im[first] * w_im[other]
                r_new = x_sum[first] * w_sum[other]
                p = p_new if p is None else p + p_new
                q = q_new if q is None else q + q_new
                r = r_new if r is None else r + r_new
            total[block, low, :] = p - q
            total[block, high, :] = r - (p + q)
        return carry

    lax.fori_loop(0, BLOCK // 8, products, 0, unroll=BLOCK // 8)
    for pair in range(blocks // 2):
        value = jnp.concatenate([total[2 * pair], total[2 * pair + 1]], axis=1)
        hi = value.astype(jnp.bfloat16)
        lo = (value - hi.astype(jnp.float32)).astype(jnp.bfloat16)
        conv = dot(inv_ref[0], hi) + (dot(inv_ref[0], lo) + dot(inv_ref[1], hi))
        conv = conv.astype(jnp.bfloat16)
        queries[2 * pair * BLOCK : (2 * pair + 1) * BLOCK, :] = conv[:, :width]
        queries[(2 * pair + 1) * BLOCK : (2 * pair + 2) * BLOCK, :] = conv[:, width:]

    reach = TILE // tok
    factor = math.log2(math.e) / math.sqrt(HEAD_DIM)
    row = lax.broadcasted_iota(jnp.int32, (2 * TILE, TILE), 1)
    col = lax.broadcasted_iota(jnp.int32, (2 * TILE, TILE), 0)
    allowed = (col <= row + TILE) & (col >= row // tok * tok)
    bias[...] = jnp.where(allowed, 0.0, -1e30)
    for tile in range(sources // reach):
        first = max(tile * reach - reach, 0)
        last = (tile + 1) * reach
        span = (last - first) * tok
        key = y_ref[first:last, tok : 2 * tok, :].reshape(span, width)
        val = y_ref[first:last, 2 * tok : 3 * tok, :].reshape(span, width)
        query = queries[tile * TILE : (tile + 1) * TILE, :]
        scores = lax.dot_general(
            key, query, (((1,), (1,)), ((), ())), preferred_element_type=jnp.float32
        )
        scores = scores + bias[2 * TILE - span :, :]
        top = jnp.max(scores, axis=0, keepdims=True)
        expo = jnp.exp2((scores - top) * factor)
        probs = (expo * (1.0 / jnp.sum(expo, axis=0, keepdims=True))).astype(jnp.bfloat16)
        mixed = lax.dot_general(
            probs, val, (((0,), (0,)), ((), ())), preferred_element_type=jnp.float32
        )
        out_ref[tile * reach : last] = mixed.astype(jnp.bfloat16).reshape(reach, tok, width)


def vmem(count):
    return [pl.BlockSpec(memory_space=pltpu.VMEM)] * count


def local(hyena_in, filt, keys, values):
    peers = lax.axis_size("context")
    tok, width = hyena_in.shape
    blocks = peers * tok // BLOCK
    hi, lo = bf16_parts(forward_table(), 2)
    fwd = jnp.asarray(np.concatenate([hi, lo], axis=1))
    inv = jnp.asarray(bf16_parts(inverse_table(), 2))
    me = lax.axis_index("context").astype(jnp.int32).reshape(1)

    packed = pack(hyena_in, keys, values, filt)
    moved = lax.all_to_all(packed, "context", split_axis=0, concat_axis=0, tiled=True)
    other = lax.ppermute(moved[:, 3 * tok :], "context", [(i, i ^ 1) for i in range(peers)])

    spectra = pl.pallas_call(
        spectra_kernel,
        out_shape=jax.ShapeDtypeStruct((blocks, 2 * BLOCK, HEAD_DIM), jnp.float32),
        in_specs=vmem(2),
        out_specs=vmem(1)[0],
        compiler_params=pltpu.CompilerParams(vmem_limit_bytes=VMEM_LIMIT),
        cost_estimate=pl.CostEstimate(flops=1 << 29, bytes_accessed=1 << 20, transcendentals=0),
        name="spectra",
    )(moved, fwd)
    mixed = pl.pallas_call(
        main_kernel,
        out_shape=jax.ShapeDtypeStruct((peers, tok, HEAD_DIM), jnp.bfloat16),
        in_specs=[pl.BlockSpec(memory_space=pltpu.SMEM)] + vmem(5),
        out_specs=vmem(1)[0],
        scratch_shapes=[
            pltpu.VMEM((blocks, 2 * BLOCK, HEAD_DIM), jnp.float32),
            pltpu.VMEM((blocks, 2 * BLOCK, HEAD_DIM), jnp.float32),
            pltpu.VMEM((peers * tok, HEAD_DIM), jnp.bfloat16),
            pltpu.VMEM((2 * TILE, TILE), jnp.float32),
            pltpu.VMEM((peers * tok, HEAD_DIM), jnp.bfloat16),
        ],
        compiler_params=pltpu.CompilerParams(vmem_limit_bytes=VMEM_LIMIT),
        cost_estimate=pl.CostEstimate(flops=5 << 30, bytes_accessed=5 << 20, transcendentals=1 << 19),
        name="conv_attention",
    )(me, moved, other, spectra, fwd, inv)
    home = lax.all_to_all(mixed, "context", split_axis=0, concat_axis=0, tiled=True)
    return home.transpose(1, 0, 2).reshape(tok, width)


def solution(mesh):
    spec = P(("dp", "context"), None)
    return jax.shard_map(
        local, mesh=mesh, in_specs=(spec,) * 4, out_specs=spec, check_vma=False
    )
```

```python
import math

import jax
import jax.numpy as jnp
import ml_dtypes
import numpy as np
from jax import lax
from jax.experimental import pallas as pl
from jax.experimental.pallas import tpu as pltpu
from jax.sharding import PartitionSpec as P

HEAD_DIM = 128
BLOCK = 256
TILE = 128
VMEM_LIMIT = 48 * 1024 * 1024
CHUNKS = 4
CONV_COST = 1024
RECURSE = False


def bf16_parts(table, count):
    parts = []
    rest = table.astype(np.float64)
    for _ in range(count):
        part = rest.astype(np.float32).astype(ml_dtypes.bfloat16)
        parts.append(part)
        rest = rest - part.astype(np.float64)
    return np.stack(parts)


def forward_table():
    freq = np.arange(BLOCK)[:, None] + 0.5
    angle = freq * np.arange(BLOCK)[None, :] * (math.pi / BLOCK)
    return np.concatenate([np.cos(angle), -np.sin(angle)], axis=0)


def inverse_table():
    freq = np.arange(BLOCK)[None, :] + 0.5
    angle = freq * (BLOCK + np.arange(BLOCK))[:, None] * (math.pi / BLOCK)
    return np.concatenate([np.cos(angle), -np.sin(angle)], axis=1) / BLOCK


def dot(left, right):
    return lax.dot_general(
        left, right, (((1,), (0,)), ((), ())), preferred_element_type=jnp.float32
    )


def copy(src, dst, sem):
    return pltpu.make_async_copy(src, dst, sem)


def pack_kernel(
    me_ref, x_ref, k_ref, v_ref, f_ref, out_ref, near_ref, far_ref, held, kept, half, load, store
):
    tok, width = x_ref.shape
    heads = width // HEAD_DIM
    group = heads // CHUNKS
    part = tok // 2
    me = me_ref[0]
    filters = copy(f_ref, half, load.at[CHUNKS])
    filters.start()
    loads = [[] for _ in range(CHUNKS)]
    loads_v = []
    for head in range(heads):
        cols = pl.ds(head * HEAD_DIM, HEAD_DIM)
        for place, ref in enumerate((x_ref, k_ref)):
            step = copy(
                ref.at[:, cols], held.at[head, pl.ds(place * tok, tok)], load.at[head // group]
            )
            step.start()
            loads[head // group].append(step)
    for head in range(heads):
        cols = pl.ds(head * HEAD_DIM, HEAD_DIM)
        apart = lax.bitwise_xor(me, jnp.int32(head))
        place = lax.bitwise_and(apart, 1) * (heads // 2) + lax.shift_right_logical(apart, 1)
        step = copy(v_ref.at[:, cols], kept.at[place], load.at[CHUNKS + 1])
        step.start()
        loads_v.append(step)
    filters.wait()
    for head in range(heads):
        first = head % 2 * part
        held[head, 2 * tok :, :] = half[first : first + part, :]
    stores = []
    for chunk in range(CHUNKS):
        for step in loads[chunk]:
            step.wait()
        some = pl.ds(chunk * group, group)
        step = copy(held.at[some], out_ref.at[some], store.at[chunk])
        step.start()
        stores.append(step)
    for step in loads_v:
        step.wait()
    for number, ref in enumerate((near_ref, far_ref)):
        step = copy(
            kept.at[pl.ds(number * (heads // 2), heads // 2)], ref, store.at[CHUNKS + number]
        )
        step.start()
        stores.append(step)
    for step in stores:
        step.wait()


def pack(me, hyena_in, keys, values, filt):
    tok, width = hyena_in.shape
    heads = width // HEAD_DIM
    shape = (heads, 2 * tok + tok // 2, HEAD_DIM)
    shape_v = (heads // 2, tok, HEAD_DIM)
    anywhere = pl.BlockSpec(memory_space=pl.ANY)
    return pl.pallas_call(
        pack_kernel,
        out_shape=[jax.ShapeDtypeStruct(some, jnp.bfloat16) for some in (shape, shape_v, shape_v)],
        in_specs=[pl.BlockSpec(memory_space=pltpu.SMEM)] + [anywhere] * 4,
        out_specs=[anywhere] * 3,
        scratch_shapes=[
            pltpu.VMEM(shape, jnp.bfloat16),
            pltpu.VMEM((heads, tok, HEAD_DIM), jnp.bfloat16),
            pltpu.VMEM((tok, HEAD_DIM), jnp.bfloat16),
            pltpu.SemaphoreType.DMA((CHUNKS + 2,)),
            pltpu.SemaphoreType.DMA((CHUNKS + 2,)),
        ],
        cost_estimate=pl.CostEstimate(
            flops=0, bytes_accessed=14 * tok * width, transcendentals=0
        ),
        name="pack",
    )(me, hyena_in, keys, values, filt)


def conv_kernel(
    me_ref,
    y_ref,
    other_ref,
    fwd_ref,
    inv_ref,
    out_ref,
    spec,
    fspec,
    filt,
    bias,
    queries,
):
    sources, _, width = y_ref.shape
    half = other_ref.shape[1]
    tok = 2 * half
    per = BLOCK // tok
    blocks = sources // per
    odd = lax.bitwise_and(me_ref[0], 1)
    for source in range(sources):
        at = pl.multiple_of(source * tok + (1 - odd) * half, half)
        filt[pl.ds(at, half), :] = other_ref[source]
    row = lax.broadcasted_iota(jnp.int32, (2 * TILE, TILE), 1)
    col = lax.broadcasted_iota(jnp.int32, (2 * TILE, TILE), 0)
    allowed = (col <= row + TILE) & (col >= row // tok * tok)
    bias[...] = jnp.where(allowed, 0.0, -1e30)
    for source in range(sources):
        at = pl.multiple_of(source * tok + odd * half, half)
        filt[pl.ds(at, half), :] = y_ref[source, 2 * tok :, :]

    for pair in range(blocks // 2):
        x_both = jnp.concatenate(
            [
                y_ref[block * per : (block + 1) * per, :tok, :].reshape(BLOCK, width)
                for block in (2 * pair, 2 * pair + 1)
            ],
            axis=1,
        )
        f_both = jnp.concatenate(
            [
                filt[block * BLOCK : (block + 1) * BLOCK, :]
                for block in (2 * pair, 2 * pair + 1)
            ],
            axis=1,
        )
        for both, result in ((x_both, spec), (f_both, fspec)):
            got = dot(fwd_ref[...], jnp.concatenate([both, both], axis=0))
            result[2 * pair] = got[:, :width]
            result[2 * pair + 1] = got[:, width:]

    sign = 1.0 - 2.0 * (lax.broadcasted_iota(jnp.int32, (8, width), 0) % 2).astype(jnp.float32)

    def products(step, carry):
        low = pl.ds(pl.multiple_of(step * 8, 8), 8)
        high = pl.ds(pl.multiple_of(step * 8 + BLOCK, 8), 8)
        x_re = [spec[block, low, :] for block in range(blocks)]
        x_im = [spec[block, high, :] for block in range(blocks)]
        x_sum = [re + im for re, im in zip(x_re, x_im)]
        f_re = [fspec[block, low, :] for block in range(blocks)]
        f_im = [fspec[block, high, :] for block in range(blocks)]
        w_re, w_im = [], []
        for block in range(blocks):
            re, im = sign * f_im[block], -sign * f_re[block]
            w_re.append(re + f_re[block - 1] if block else re)
            w_im.append(im + f_im[block - 1] if block else im)
        w_sum = [re + im for re, im in zip(w_re, w_im)]
        for block in range(blocks):
            p = q = r = None
            for first in range(block + 1):
                other = block - first
                p_new = x_re[first] * w_re[other]
                q_new = x_im[first] * w_im[other]
                r_new = x_sum[first] * w_sum[other]
                p = p_new if p is None else p + p_new
                q = q_new if q is None else q + q_new
                r = r_new if r is None else r + r_new
            spec[block, low, :] = p - q
            spec[block, high, :] = r - (p + q)
        return carry

    lax.fori_loop(0, BLOCK // 8, products, 0, unroll=BLOCK // 8)
    for pair in range(blocks // 2):
        value = jnp.concatenate([spec[2 * pair], spec[2 * pair + 1]], axis=1)
        hi = value.astype(jnp.bfloat16)
        lo = (value - hi.astype(jnp.float32)).astype(jnp.bfloat16)
        conv = dot(inv_ref[0], hi) + (dot(inv_ref[0], lo) + dot(inv_ref[1], hi))
        conv = conv.astype(jnp.bfloat16)
        queries[2 * pair * BLOCK : (2 * pair + 1) * BLOCK, :] = conv[:, :width]
        queries[(2 * pair + 1) * BLOCK : (2 * pair + 2) * BLOCK, :] = conv[:, width:]

    reach = TILE // tok
    factor = math.log2(math.e) / math.sqrt(HEAD_DIM)
    for tile in range(sources // reach):
        first = max(tile * reach - reach, 0)
        last = (tile + 1) * reach
        span = (last - first) * tok
        key = y_ref[first:last, tok : 2 * tok, :].reshape(span, width)
        query = queries[tile * TILE : (tile + 1) * TILE, :]
        scores = lax.dot_general(
            key, query, (((1,), (1,)), ((), ())), preferred_element_type=jnp.float32
        )
        scores = scores + bias[2 * TILE - span :, :]
        top = jnp.max(scores, axis=0, keepdims=True)
        expo = jnp.exp2((scores - top) * factor)
        probs = expo * (1.0 / jnp.sum(expo, axis=0, keepdims=True))
        out_ref[tile, 2 * TILE - span :, :] = probs.astype(jnp.bfloat16)


def mix_kernel(me_ref, probs_ref, *refs):
    pieces, out_ref, val = refs[:-2], refs[-2], refs[-1]
    sources, tok, width = val.shape
    me = me_ref[0]
    for along_z, ref in enumerate(pieces):
        for core in range(2):
            for along_x in range(ref.shape[1]):
                apart = along_x * 8 + along_z * 2 + core
                val[lax.bitwise_xor(me, jnp.int32(apart))] = ref[core, along_x]
    reach = TILE // tok
    for tile in range(sources // reach):
        first = max(tile * reach - reach, 0)
        last = (tile + 1) * reach
        span = (last - first) * tok
        mixed = lax.dot_general(
            probs_ref[tile, 2 * TILE - span :, :],
            val[first:last].reshape(span, width),
            (((0,), (0,)), ((), ())),
            preferred_element_type=jnp.float32,
        )
        out_ref[tile * reach : last] = mixed.astype(jnp.bfloat16).reshape(reach, tok, width)


def vmem(count):
    return [pl.BlockSpec(memory_space=pltpu.VMEM)] * count


def swap(array, bits):
    peers = lax.axis_size("context")
    return lax.ppermute(array, "context", [(i, i ^ bits) for i in range(peers)])


def route(near, far):
    _, tok, width = near.shape
    near = near.reshape(4, 4, tok, width)
    other = swap(far, 1).reshape(4, 4, tok, width)
    if RECURSE:
        both = jnp.stack([near, other])
        step = swap(jnp.stack([both[:, 1], both[:, 3]]), 8)
        last = swap(jnp.stack([both[:, 2], step[1]]), 16)
        arrived = [both[:, 0], step[0], last[0], last[1]]
    else:
        arrived = []
        for along_x in range(4):
            both = jnp.stack([near[along_x], other[along_x]])
            arrived.append(swap(both, along_x * 8) if along_x else both)
    pieces = []
    for along_z in range(4):
        mine = jnp.stack([some[:, along_z] for some in arrived], axis=1)
        pieces.append(swap(mine, along_z * 2) if along_z else mine)
    return pieces


def local(hyena_in, filt, keys, values):
    peers = lax.axis_size("context")
    tok, width = hyena_in.shape
    blocks = peers * tok // BLOCK
    tiles = peers * tok // TILE
    hi, lo = bf16_parts(forward_table(), 2)
    fwd = jnp.asarray(np.concatenate([hi, lo], axis=1))
    inv = jnp.asarray(bf16_parts(inverse_table(), 2))
    me = lax.axis_index("context").astype(jnp.int32).reshape(1)
    params = pltpu.CompilerParams(vmem_limit_bytes=VMEM_LIMIT)
    scalar = pl.BlockSpec(memory_space=pltpu.SMEM)

    packed, near, far = pack(me, hyena_in, keys, values, filt)
    moved = lax.all_to_all(packed, "context", split_axis=0, concat_axis=0, tiled=True)
    pieces = route(near, far)
    mine = moved[:, 2 * tok :]
    pairs = [[i, i + 1] for i in range(0, peers, 2)]
    both = lax.all_to_all(jnp.stack([mine, mine]), "context", 0, 0, axis_index_groups=pairs, tiled=True)
    other = jnp.where(me[0] % 2 == 1, both[0], both[1])

    probs = pl.pallas_call(
        conv_kernel,
        out_shape=jax.ShapeDtypeStruct((tiles, 2 * TILE, TILE), jnp.bfloat16),
        in_specs=[scalar] + vmem(4),
        out_specs=vmem(1)[0],
        scratch_shapes=[
            pltpu.VMEM((blocks, 2 * BLOCK, HEAD_DIM), jnp.float32),
            pltpu.VMEM((blocks, 2 * BLOCK, HEAD_DIM), jnp.float32),
            pltpu.VMEM((peers * tok, HEAD_DIM), jnp.bfloat16),
            pltpu.VMEM((2 * TILE, TILE), jnp.float32),
            pltpu.VMEM((peers * tok, HEAD_DIM), jnp.bfloat16),
        ],
        compiler_params=params,
        cost_estimate=pl.CostEstimate(flops=5 << 30, bytes_accessed=5 << 20, transcendentals=1 << 19),
        name="conv_probs",
    )(me, moved, other, fwd, inv)
    mixed = pl.pallas_call(
        mix_kernel,
        out_shape=jax.ShapeDtypeStruct((peers, tok, HEAD_DIM), jnp.bfloat16),
        in_specs=[scalar] + vmem(5),
        out_specs=vmem(1)[0],
        scratch_shapes=[pltpu.VMEM((peers, tok, HEAD_DIM), jnp.bfloat16)],
        compiler_params=params,
        cost_estimate=pl.CostEstimate(flops=1 << 28, bytes_accessed=2 << 20, transcendentals=0),
        name="mix",
    )(me, probs, *pieces)
    home = lax.all_to_all(mixed, "context", split_axis=0, concat_axis=0, tiled=True)
    return home.transpose(1, 0, 2).reshape(tok, width)


def solution(mesh):
    spec = P(("dp", "context"), None)
    return jax.shard_map(
        local, mesh=mesh, in_specs=(spec,) * 4, out_specs=spec, check_vma=False
    )
```

```python
import math

import jax
import jax.numpy as jnp
import ml_dtypes
import numpy as np
from jax import lax
from jax.experimental import pallas as pl
from jax.experimental.pallas import tpu as pltpu
from jax.sharding import PartitionSpec as P

HEAD_DIM = 128
BLOCK = 256
TILE = 128
VMEM_LIMIT = 48 * 1024 * 1024
CHUNKS = 4
EARLY = 16
ORDER_X = (0, 3, 2, 1)
ORDER_Z = (0, 2, 3, 1)


def bf16_parts(table, count):
    parts = []
    rest = table.astype(np.float64)
    for _ in range(count):
        part = rest.astype(np.float32).astype(ml_dtypes.bfloat16)
        parts.append(part)
        rest = rest - part.astype(np.float64)
    return np.stack(parts)


def forward_table():
    freq = np.arange(BLOCK)[:, None] + 0.5
    angle = freq * np.arange(BLOCK)[None, :] * (math.pi / BLOCK)
    return np.concatenate([np.cos(angle), -np.sin(angle)], axis=0)


def inverse_table():
    freq = np.arange(BLOCK)[None, :] + 0.5
    angle = freq * (BLOCK + np.arange(BLOCK))[:, None] * (math.pi / BLOCK)
    return np.concatenate([np.cos(angle), -np.sin(angle)], axis=1) / BLOCK


def dot(left, right):
    return lax.dot_general(
        left, right, (((1,), (0,)), ((), ())), preferred_element_type=jnp.float32
    )


def copy(src, dst, sem):
    return pltpu.make_async_copy(src, dst, sem)


def pack_kernel(
    me_ref, x_ref, k_ref, v_ref, f_ref, out_ref, near_ref, far_ref, held, kept, half, load, store
):
    tok, width = x_ref.shape
    heads = width // HEAD_DIM
    group = heads // CHUNKS
    part = tok // 2
    me = me_ref[0]
    filters = copy(f_ref, half, load.at[CHUNKS])
    filters.start()
    loads = [[] for _ in range(CHUNKS)]
    loads_v = []
    for head in range(heads):
        cols = pl.ds(head * HEAD_DIM, HEAD_DIM)
        parts = [
            (x_ref.at[:, cols], pl.ds(0, tok)),
            (k_ref.at[:, cols], pl.ds(tok, tok)),
            (v_ref.at[pl.ds(0, EARLY), cols], pl.ds(2 * tok + part, EARLY)),
        ]
        for source, rows in parts:
            step = copy(source, held.at[head, rows], load.at[head // group])
            step.start()
            loads[head // group].append(step)
    for head in range(heads):
        cols = pl.ds(head * HEAD_DIM, HEAD_DIM)
        apart = lax.bitwise_xor(me, jnp.int32(head))
        place = lax.bitwise_and(apart, 1) * (heads // 2) + lax.shift_right_logical(apart, 1)
        step = copy(
            v_ref.at[pl.ds(EARLY, tok - EARLY), cols], kept.at[place], load.at[CHUNKS + 1]
        )
        step.start()
        loads_v.append(step)
    filters.wait()
    for head in range(heads):
        first = head % 2 * part
        held[head, 2 * tok : 2 * tok + part, :] = half[first : first + part, :]
    stores = []
    for chunk in range(CHUNKS):
        for step in loads[chunk]:
            step.wait()
        some = pl.ds(chunk * group, group)
        step = copy(held.at[some], out_ref.at[some], store.at[chunk])
        step.start()
        stores.append(step)
    for step in loads_v:
        step.wait()
    for number, ref in enumerate((near_ref, far_ref)):
        step = copy(
            kept.at[pl.ds(number * (heads // 2), heads // 2)], ref, store.at[CHUNKS + number]
        )
        step.start()
        stores.append(step)
    for step in stores:
        step.wait()


def pack(me, hyena_in, keys, values, filt):
    tok, width = hyena_in.shape
    heads = width // HEAD_DIM
    shape = (heads, 2 * tok + tok // 2 + EARLY, HEAD_DIM)
    shape_v = (heads // 2, tok - EARLY, HEAD_DIM)
    anywhere = pl.BlockSpec(memory_space=pl.ANY)
    return pl.pallas_call(
        pack_kernel,
        out_shape=[jax.ShapeDtypeStruct(some, jnp.bfloat16) for some in (shape, shape_v, shape_v)],
        in_specs=[pl.BlockSpec(memory_space=pltpu.SMEM)] + [anywhere] * 4,
        out_specs=[anywhere] * 3,
        scratch_shapes=[
            pltpu.VMEM(shape, jnp.bfloat16),
            pltpu.VMEM((heads, tok - EARLY, HEAD_DIM), jnp.bfloat16),
            pltpu.VMEM((tok, HEAD_DIM), jnp.bfloat16),
            pltpu.SemaphoreType.DMA((CHUNKS + 2,)),
            pltpu.SemaphoreType.DMA((CHUNKS + 2,)),
        ],
        cost_estimate=pl.CostEstimate(
            flops=0, bytes_accessed=14 * tok * width, transcendentals=0
        ),
        name="pack",
    )(me, hyena_in, keys, values, filt)


def spectra(halves, table, result):
    width = result.shape[2]
    rows = BLOCK // 2
    first, second = halves
    for pair in range(result.shape[0] // 2):
        both = [
            jnp.concatenate(
                [half[block].reshape(rows, width) for block in (2 * pair, 2 * pair + 1)], axis=1
            )
            for half in (first, second)
        ]
        got = dot(table, jnp.concatenate(both + both, axis=0))
        result[2 * pair] = got[:, :width]
        result[2 * pair + 1] = got[:, width:]


def conv_kernel(
    y_ref, filt_ref, fwd_ref, inv_ref, out_ref, spec, fspec, bias, queries
):
    sources, _, width = y_ref.shape
    half = filt_ref.shape[2]
    tok = 2 * half
    per = BLOCK // tok
    blocks = sources // per
    groups = [slice(first, first + per) for first in range(0, sources, per)]
    spectra(
        [[y_ref[some, :half, :] for some in groups], [y_ref[some, half:tok, :] for some in groups]],
        fwd_ref[...],
        spec,
    )
    spectra(
        [[filt_ref[part, some] for some in groups] for part in range(2)], fwd_ref[...], fspec
    )

    sign = 1.0 - 2.0 * (lax.broadcasted_iota(jnp.int32, (8, width), 0) % 2).astype(jnp.float32)

    def products(step, carry):
        low = pl.ds(pl.multiple_of(step * 8, 8), 8)
        high = pl.ds(pl.multiple_of(step * 8 + BLOCK, 8), 8)
        x_re = [spec[block, low, :] for block in range(blocks)]
        x_im = [spec[block, high, :] for block in range(blocks)]
        x_sum = [re + im for re, im in zip(x_re, x_im)]
        f_re = [fspec[block, low, :] for block in range(blocks)]
        f_im = [fspec[block, high, :] for block in range(blocks)]
        w_re, w_im = [], []
        for block in range(blocks):
            re, im = sign * f_im[block], -sign * f_re[block]
            w_re.append(re + f_re[block - 1] if block else re)
            w_im.append(im + f_im[block - 1] if block else im)
        w_sum = [re + im for re, im in zip(w_re, w_im)]
        for block in range(blocks):
            p = q = r = None
            for first in range(block + 1):
                other = block - first
                p_new = x_re[first] * w_re[other]
                q_new = x_im[first] * w_im[other]
                r_new = x_sum[first] * w_sum[other]
                p = p_new if p is None else p + p_new
                q = q_new if q is None else q + q_new
                r = r_new if r is None else r + r_new
            spec[block, low, :] = p - q
            spec[block, high, :] = r - (p + q)
        return carry

    lax.fori_loop(0, BLOCK // 8, products, 0, unroll=BLOCK // 8)
    for pair in range(blocks // 2):
        value = jnp.concatenate([spec[2 * pair], spec[2 * pair + 1]], axis=1)
        hi = value.astype(jnp.bfloat16)
        lo = (value - hi.astype(jnp.float32)).astype(jnp.bfloat16)
        conv = dot(inv_ref[0], hi) + (dot(inv_ref[0], lo) + dot(inv_ref[1], hi))
        conv = conv.astype(jnp.bfloat16)
        queries[2 * pair * BLOCK : (2 * pair + 1) * BLOCK, :] = conv[:, :width]
        queries[(2 * pair + 1) * BLOCK : (2 * pair + 2) * BLOCK, :] = conv[:, width:]

    reach = TILE // tok
    factor = math.log2(math.e) / math.sqrt(HEAD_DIM)
    row = lax.broadcasted_iota(jnp.int32, (2 * TILE, TILE), 1)
    col = lax.broadcasted_iota(jnp.int32, (2 * TILE, TILE), 0)
    allowed = (col <= row + TILE) & (col >= row // tok * tok)
    bias[...] = jnp.where(allowed, 0.0, -1e30)
    for tile in range(sources // reach):
        first = max(tile * reach - reach, 0)
        last = (tile + 1) * reach
        span = (last - first) * tok
        key = y_ref[first:last, tok : 2 * tok, :].reshape(span, width)
        query = queries[tile * TILE : (tile + 1) * TILE, :]
        scores = lax.dot_general(
            key, query, (((1,), (1,)), ((), ())), preferred_element_type=jnp.float32
        )
        scores = scores + bias[2 * TILE - span :, :]
        top = jnp.max(scores, axis=0, keepdims=True)
        expo = jnp.exp2((scores - top) * factor)
        probs = expo * (1.0 / jnp.sum(expo, axis=0, keepdims=True))
        out_ref[tile, 2 * TILE - span :, :] = probs.astype(jnp.bfloat16)


def mix_kernel(me_ref, probs_ref, y_ref, *refs):
    pieces, out_ref, val = refs[:-2], refs[-2], refs[-1]
    sources, tok, width = val.shape
    me = me_ref[0]
    for source in range(sources):
        val[source, :EARLY, :] = y_ref[source, 2 * tok + tok // 2 :, :]
    for along_z, ref in enumerate(pieces):
        for core in range(2):
            for along_x in range(ref.shape[1]):
                apart = ORDER_X[along_x] * 8 + ORDER_Z[along_z] * 2 + core
                val[lax.bitwise_xor(me, jnp.int32(apart)), EARLY:, :] = ref[core, along_x]
    reach = TILE // tok
    for tile in range(sources // reach):
        first = max(tile * reach - reach, 0)
        last = (tile + 1) * reach
        span = (last - first) * tok
        mixed = lax.dot_general(
            probs_ref[tile, 2 * TILE - span :, :],
            val[first:last].reshape(span, width),
            (((0,), (0,)), ((), ())),
            preferred_element_type=jnp.float32,
        )
        out_ref[tile * reach : last] = mixed.astype(jnp.bfloat16).reshape(reach, tok, width)


def vmem(count):
    return [pl.BlockSpec(memory_space=pltpu.VMEM)] * count


def swap(array, bits):
    peers = lax.axis_size("context")
    return lax.ppermute(array, "context", [(i, i ^ bits) for i in range(peers)])


def route(near, far):
    _, tok, width = near.shape
    near = near.reshape(4, 4, tok, width)
    other = swap(far, 1).reshape(4, 4, tok, width)
    arrived = []
    for along_x in range(4):
        both = jnp.stack([near[along_x], other[along_x]])
        arrived.append(swap(both, along_x * 8) if along_x else both)
    pieces = []
    for along_z in ORDER_Z:
        mine = jnp.stack([arrived[x][:, along_z] for x in ORDER_X], axis=1)
        pieces.append(swap(mine, along_z * 2) if along_z else mine)
    return pieces


def local(hyena_in, filt, keys, values):
    peers = lax.axis_size("context")
    tok, width = hyena_in.shape
    blocks = peers * tok // BLOCK
    tiles = peers * tok // TILE
    hi, lo = bf16_parts(forward_table(), 2)
    place = np.arange(BLOCK) % tok // (tok // 2)
    order = np.concatenate([np.flatnonzero(place == 0), np.flatnonzero(place == 1)])
    fwd = jnp.asarray(np.concatenate([hi[:, order], lo[:, order]], axis=1))
    inv = jnp.asarray(bf16_parts(inverse_table(), 2))
    me = lax.axis_index("context").astype(jnp.int32).reshape(1)
    params = pltpu.CompilerParams(vmem_limit_bytes=VMEM_LIMIT)
    scalar = pl.BlockSpec(memory_space=pltpu.SMEM)

    packed, near, far = pack(me, hyena_in, keys, values, filt)
    moved = lax.all_to_all(packed, "context", split_axis=0, concat_axis=0, tiled=True)
    pieces = route(near, far)
    half = moved[:, 2 * tok : 2 * tok + tok // 2]
    pairs = [[i, i + 1] for i in range(0, peers, 2)]
    filters = lax.all_gather(half, "context", axis_index_groups=pairs, axis=0, tiled=False)

    probs = pl.pallas_call(
        conv_kernel,
        out_shape=jax.ShapeDtypeStruct((tiles, 2 * TILE, TILE), jnp.bfloat16),
        in_specs=vmem(4),
        out_specs=vmem(1)[0],
        scratch_shapes=[
            pltpu.VMEM((blocks, 2 * BLOCK, HEAD_DIM), jnp.float32),
            pltpu.VMEM((blocks, 2 * BLOCK, HEAD_DIM), jnp.float32),
            pltpu.VMEM((2 * TILE, TILE), jnp.float32),
            pltpu.VMEM((peers * tok, HEAD_DIM), jnp.bfloat16),
        ],
        compiler_params=params,
        cost_estimate=pl.CostEstimate(flops=5 << 30, bytes_accessed=5 << 20, transcendentals=1 << 19),
        name="conv_probs",
    )(moved, filters, fwd, inv)
    mixed = pl.pallas_call(
        mix_kernel,
        out_shape=jax.ShapeDtypeStruct((peers, tok, HEAD_DIM), jnp.bfloat16),
        in_specs=[scalar] + vmem(6),
        out_specs=vmem(1)[0],
        scratch_shapes=[pltpu.VMEM((peers, tok, HEAD_DIM), jnp.bfloat16)],
        compiler_params=params,
        cost_estimate=pl.CostEstimate(flops=1 << 28, bytes_accessed=2 << 20, transcendentals=0),
        name="mix",
    )(me, probs, moved, *pieces)
    home = lax.all_to_all(mixed, "context", split_axis=0, concat_axis=0, tiled=True)
    return home.transpose(1, 0, 2).reshape(tok, width)


def solution(mesh):
    spec = P(("dp", "context"), None)
    return jax.shard_map(
        local, mesh=mesh, in_specs=(spec,) * 4, out_specs=spec, check_vma=False
    )
```

```python
import math

import jax
import jax.numpy as jnp
import ml_dtypes
import numpy as np
from jax import lax
from jax.experimental import pallas as pl
from jax.experimental.pallas import tpu as pltpu
from jax.sharding import PartitionSpec as P

HEAD_DIM = 128
BLOCK = 256
TILE = 128
VMEM_LIMIT = 48 * 1024 * 1024
CHUNKS = 4
EARLY = 16
ORDER_X = (0, 3, 2, 1)
ORDER_Z = (0, 2, 3, 1)


def bf16_parts(table, count):
    parts = []
    rest = table.astype(np.float64)
    for _ in range(count):
        part = rest.astype(np.float32).astype(ml_dtypes.bfloat16)
        parts.append(part)
        rest = rest - part.astype(np.float64)
    return np.stack(parts)


def forward_table():
    freq = np.arange(BLOCK)[:, None] + 0.5
    angle = freq * np.arange(BLOCK)[None, :] * (math.pi / BLOCK)
    return np.concatenate([np.cos(angle), -np.sin(angle)], axis=0)


def inverse_table():
    freq = np.arange(BLOCK)[None, :] + 0.5
    angle = freq * (BLOCK + np.arange(BLOCK))[:, None] * (math.pi / BLOCK)
    return np.concatenate([np.cos(angle), -np.sin(angle)], axis=1) / BLOCK


def dot(left, right):
    return lax.dot_general(
        left, right, (((1,), (0,)), ((), ())), preferred_element_type=jnp.float32
    )


def copy(src, dst, sem):
    return pltpu.make_async_copy(src, dst, sem)


def pack_kernel(
    me_ref, x_ref, k_ref, v_ref, f_ref, out_ref, near_ref, far_ref, held, kept, half, load, store
):
    tok, width = x_ref.shape
    heads = width // HEAD_DIM
    group = heads // CHUNKS
    part = tok // 4
    me = me_ref[0]
    filters = copy(f_ref, half, load.at[CHUNKS])
    filters.start()
    loads = [[] for _ in range(CHUNKS)]
    loads_v = []
    for head in range(heads):
        cols = pl.ds(head * HEAD_DIM, HEAD_DIM)
        parts = [
            (x_ref.at[:, cols], pl.ds(0, tok)),
            (k_ref.at[:, cols], pl.ds(tok, tok)),
            (v_ref.at[pl.ds(0, EARLY), cols], pl.ds(2 * tok + part, EARLY)),
        ]
        for source, rows in parts:
            step = copy(source, held.at[head, rows], load.at[head // group])
            step.start()
            loads[head // group].append(step)
    for head in range(heads):
        cols = pl.ds(head * HEAD_DIM, HEAD_DIM)
        apart = lax.bitwise_xor(me, jnp.int32(head))
        place = lax.bitwise_and(apart, 1) * (heads // 2) + lax.shift_right_logical(apart, 1)
        step = copy(
            v_ref.at[pl.ds(EARLY, tok - EARLY), cols], kept.at[place], load.at[CHUNKS + 1]
        )
        step.start()
        loads_v.append(step)
    filters.wait()
    for head in range(heads):
        first = (head // 8 % 2 * 2 + head % 2) * part
        held[head, 2 * tok : 2 * tok + part, :] = half[first : first + part, :]
    stores = []
    for chunk in range(CHUNKS):
        for step in loads[chunk]:
            step.wait()
        some = pl.ds(chunk * group, group)
        step = copy(held.at[some], out_ref.at[some], store.at[chunk])
        step.start()
        stores.append(step)
    for step in loads_v:
        step.wait()
    for number, ref in enumerate((near_ref, far_ref)):
        step = copy(
            kept.at[pl.ds(number * (heads // 2), heads // 2)], ref, store.at[CHUNKS + number]
        )
        step.start()
        stores.append(step)
    for step in stores:
        step.wait()


def pack(me, hyena_in, keys, values, filt):
    tok, width = hyena_in.shape
    heads = width // HEAD_DIM
    shape = (heads, 2 * tok + tok // 4 + EARLY, HEAD_DIM)
    shape_v = (heads // 2, tok - EARLY, HEAD_DIM)
    anywhere = pl.BlockSpec(memory_space=pl.ANY)
    return pl.pallas_call(
        pack_kernel,
        out_shape=[jax.ShapeDtypeStruct(some, jnp.bfloat16) for some in (shape, shape_v, shape_v)],
        in_specs=[pl.BlockSpec(memory_space=pltpu.SMEM)] + [anywhere] * 4,
        out_specs=[anywhere] * 3,
        scratch_shapes=[
            pltpu.VMEM(shape, jnp.bfloat16),
            pltpu.VMEM((heads, tok - EARLY, HEAD_DIM), jnp.bfloat16),
            pltpu.VMEM((tok, HEAD_DIM), jnp.bfloat16),
            pltpu.SemaphoreType.DMA((CHUNKS + 2,)),
            pltpu.SemaphoreType.DMA((CHUNKS + 2,)),
        ],
        cost_estimate=pl.CostEstimate(
            flops=0, bytes_accessed=14 * tok * width, transcendentals=0
        ),
        name="pack",
    )(me, hyena_in, keys, values, filt)


def spectra(halves, table, result):
    width = result.shape[2]
    rows = BLOCK // len(halves)
    for pair in range(result.shape[0] // 2):
        both = [
            jnp.concatenate(
                [half[block].reshape(rows, width) for block in (2 * pair, 2 * pair + 1)], axis=1
            )
            for half in halves
        ]
        got = dot(table, jnp.concatenate(both + both, axis=0))
        result[2 * pair] = got[:, :width]
        result[2 * pair + 1] = got[:, width:]


def conv_kernel(
    y_ref, filt_ref, fwd_ref, inv_ref, out_ref, spec, fspec, bias, queries
):
    sources, _, width = y_ref.shape
    part = filt_ref.shape[2]
    tok = 4 * part
    per = BLOCK // tok
    blocks = sources // per
    groups = [slice(first, first + per) for first in range(0, sources, per)]
    spectra(
        [[y_ref[some, q * part : (q + 1) * part, :] for some in groups] for q in range(4)],
        fwd_ref[...],
        spec,
    )
    spectra([[filt_ref[q, some] for some in groups] for q in range(4)], fwd_ref[...], fspec)

    sign = 1.0 - 2.0 * (lax.broadcasted_iota(jnp.int32, (8, width), 0) % 2).astype(jnp.float32)

    def products(step, carry):
        low = pl.ds(pl.multiple_of(step * 8, 8), 8)
        high = pl.ds(pl.multiple_of(step * 8 + BLOCK, 8), 8)
        x_re = [spec[block, low, :] for block in range(blocks)]
        x_im = [spec[block, high, :] for block in range(blocks)]
        x_sum = [re + im for re, im in zip(x_re, x_im)]
        f_re = [fspec[block, low, :] for block in range(blocks)]
        f_im = [fspec[block, high, :] for block in range(blocks)]
        w_re, w_im = [], []
        for block in range(blocks):
            re, im = sign * f_im[block], -sign * f_re[block]
            w_re.append(re + f_re[block - 1] if block else re)
            w_im.append(im + f_im[block - 1] if block else im)
        w_sum = [re + im for re, im in zip(w_re, w_im)]
        for block in range(blocks):
            p = q = r = None
            for first in range(block + 1):
                other = block - first
                p_new = x_re[first] * w_re[other]
                q_new = x_im[first] * w_im[other]
                r_new = x_sum[first] * w_sum[other]
                p = p_new if p is None else p + p_new
                q = q_new if q is None else q + q_new
                r = r_new if r is None else r + r_new
            spec[block, low, :] = p - q
            spec[block, high, :] = r - (p + q)
        return carry

    lax.fori_loop(0, BLOCK // 8, products, 0, unroll=BLOCK // 8)
    for pair in range(blocks // 2):
        value = jnp.concatenate([spec[2 * pair], spec[2 * pair + 1]], axis=1)
        hi = value.astype(jnp.bfloat16)
        lo = (value - hi.astype(jnp.float32)).astype(jnp.bfloat16)
        conv = dot(inv_ref[0], hi) + (dot(inv_ref[0], lo) + dot(inv_ref[1], hi))
        conv = conv.astype(jnp.bfloat16)
        queries[2 * pair * BLOCK : (2 * pair + 1) * BLOCK, :] = conv[:, :width]
        queries[(2 * pair + 1) * BLOCK : (2 * pair + 2) * BLOCK, :] = conv[:, width:]

    reach = TILE // tok
    factor = math.log2(math.e) / math.sqrt(HEAD_DIM)
    row = lax.broadcasted_iota(jnp.int32, (2 * TILE, TILE), 1)
    col = lax.broadcasted_iota(jnp.int32, (2 * TILE, TILE), 0)
    allowed = (col <= row + TILE) & (col >= row // tok * tok)
    bias[...] = jnp.where(allowed, 0.0, -1e30)
    for tile in range(sources // reach):
        first = max(tile * reach - reach, 0)
        last = (tile + 1) * reach
        span = (last - first) * tok
        key = y_ref[first:last, tok : 2 * tok, :].reshape(span, width)
        query = queries[tile * TILE : (tile + 1) * TILE, :]
        scores = lax.dot_general(
            key, query, (((1,), (1,)), ((), ())), preferred_element_type=jnp.float32
        )
        scores = scores + bias[2 * TILE - span :, :]
        top = jnp.max(scores, axis=0, keepdims=True)
        expo = jnp.exp2((scores - top) * factor)
        probs = expo * (1.0 / jnp.sum(expo, axis=0, keepdims=True))
        out_ref[tile, 2 * TILE - span :, :] = probs.astype(jnp.bfloat16)


def mix_kernel(me_ref, probs_ref, y_ref, *refs):
    pieces, out_ref, val = refs[:-2], refs[-2], refs[-1]
    sources, tok, width = val.shape
    me = me_ref[0]
    for source in range(sources):
        val[source, :EARLY, :] = y_ref[source, 2 * tok + tok // 4 :, :]
    for along_z, ref in enumerate(pieces):
        for core in range(2):
            for along_x in range(ref.shape[1]):
                apart = ORDER_X[along_x] * 8 + ORDER_Z[along_z] * 2 + core
                val[lax.bitwise_xor(me, jnp.int32(apart)), EARLY:, :] = ref[core, along_x]
    reach = TILE // tok
    for tile in range(sources // reach):
        first = max(tile * reach - reach, 0)
        last = (tile + 1) * reach
        span = (last - first) * tok
        mixed = lax.dot_general(
            probs_ref[tile, 2 * TILE - span :, :],
            val[first:last].reshape(span, width),
            (((0,), (0,)), ((), ())),
            preferred_element_type=jnp.float32,
        )
        out_ref[tile * reach : last] = mixed.astype(jnp.bfloat16).reshape(reach, tok, width)


def vmem(count):
    return [pl.BlockSpec(memory_space=pltpu.VMEM)] * count


def swap(array, bits):
    peers = lax.axis_size("context")
    return lax.ppermute(array, "context", [(i, i ^ bits) for i in range(peers)])


def route(near, far):
    _, tok, width = near.shape
    near = near.reshape(4, 4, tok, width)
    other = swap(far, 1).reshape(4, 4, tok, width)
    arrived = []
    for along_x in range(4):
        both = jnp.stack([near[along_x], other[along_x]])
        arrived.append(swap(both, along_x * 8) if along_x else both)
    pieces = []
    for along_z in ORDER_Z:
        mine = jnp.stack([arrived[x][:, along_z] for x in ORDER_X], axis=1)
        pieces.append(swap(mine, along_z * 2) if along_z else mine)
    return pieces


def local(hyena_in, filt, keys, values):
    peers = lax.axis_size("context")
    tok, width = hyena_in.shape
    blocks = peers * tok // BLOCK
    tiles = peers * tok // TILE
    hi, lo = bf16_parts(forward_table(), 2)
    place = np.arange(BLOCK) % tok // (tok // 4)
    order = np.concatenate([np.flatnonzero(place == q) for q in range(4)])
    fwd = jnp.asarray(np.concatenate([hi[:, order], lo[:, order]], axis=1))
    inv = jnp.asarray(bf16_parts(inverse_table(), 2))
    me = lax.axis_index("context").astype(jnp.int32).reshape(1)
    params = pltpu.CompilerParams(vmem_limit_bytes=VMEM_LIMIT)
    scalar = pl.BlockSpec(memory_space=pltpu.SMEM)

    packed, near, far = pack(me, hyena_in, keys, values, filt)
    moved = lax.all_to_all(packed, "context", split_axis=0, concat_axis=0, tiled=True)
    pieces = route(near, far)
    quarter = moved[:, 2 * tok : 2 * tok + tok // 4]
    fours = [[i, i + 1, i + 8, i + 9] for i in range(0, peers, 2) if i // 8 % 2 == 0]
    filters = lax.all_gather(quarter, "context", axis_index_groups=fours, axis=0, tiled=False)

    probs = pl.pallas_call(
        conv_kernel,
        out_shape=jax.ShapeDtypeStruct((tiles, 2 * TILE, TILE), jnp.bfloat16),
        in_specs=vmem(4),
        out_specs=vmem(1)[0],
        scratch_shapes=[
            pltpu.VMEM((blocks, 2 * BLOCK, HEAD_DIM), jnp.float32),
            pltpu.VMEM((blocks, 2 * BLOCK, HEAD_DIM), jnp.float32),
            pltpu.VMEM((2 * TILE, TILE), jnp.float32),
            pltpu.VMEM((peers * tok, HEAD_DIM), jnp.bfloat16),
        ],
        compiler_params=params,
        cost_estimate=pl.CostEstimate(flops=5 << 30, bytes_accessed=5 << 20, transcendentals=1 << 19),
        name="conv_probs",
    )(moved, filters, fwd, inv)
    mixed = pl.pallas_call(
        mix_kernel,
        out_shape=jax.ShapeDtypeStruct((peers, tok, HEAD_DIM), jnp.bfloat16),
        in_specs=[scalar] + vmem(6),
        out_specs=vmem(1)[0],
        scratch_shapes=[pltpu.VMEM((peers, tok, HEAD_DIM), jnp.bfloat16)],
        compiler_params=params,
        cost_estimate=pl.CostEstimate(flops=1 << 28, bytes_accessed=2 << 20, transcendentals=0),
        name="mix",
    )(me, probs, moved, *pieces)
    home = lax.all_to_all(mixed, "context", split_axis=0, concat_axis=0, tiled=True)
    return home.transpose(1, 0, 2).reshape(tok, width)


def solution(mesh):
    spec = P(("dp", "context"), None)
    return jax.shard_map(
        local, mesh=mesh, in_specs=(spec,) * 4, out_specs=spec, check_vma=False
    )
```
